256 devices in a mesh: bulk: 16 (over y, z_hi, core), occ: 16 (over x, z_lo).
Axes of the slice: x: 4, y: 4, z: 8 (z_hi: 2, z_lo: 4; z = z_hi * 4 + z_lo), core: 2. Of those that a mesh axis runs over, the one named last changes fastest.
Arguments:
- lambda_cd: bfloat16 [512, 256, 900], P('bulk', 'occ'), may hold values from -6 to 6
- integrals: bfloat16 [256, 900, 4096], P('occ', None, 'bulk'), may hold values from -0.01171875 to 0.01171875
- other_terms: bfloat16 [512, 4096], P('occ', 'bulk'), may hold values from -6 to 6
- hole_energy: float32 [60], replicated, may hold values from 0.3 to 3
- virtual_energy: float32 [64], replicated, may hold values from 0.1 to 3
- pair_orbitals: int32 [512, 2], P('occ'), may hold values from 0 to 59
Outputs:
- new_lambda: float32 [512, 4096], P('occ', 'bulk')
The draws below stay inside these ranges and needn't reach their ends.
All inputs are finite; a program needn't handle non-finite values.
Results may differ from the reference program's by a relative error of at most 0.0003.
Values may be sent and summed in bfloat16 or wider, within the bound.
No kernel may reach another device: no remote copies, remote signals or barrier semaphores. Data moves between devices by JAX's collectives and lax.ppermute only.
A program may use at most 128 MiB of HBM per device.

```python
import math
import jax
import jax.numpy as jnp

NOCC = 60
V = 900
NC = 256
VW = 64
IJ = 512
AB = 4096


def with_ends(array, key, smallest, high):
    longest = array.shape.index(max(array.shape))
    spots = []
    for shift in (0, 1):
        where = [jax.random.randint(jax.random.fold_in(key, axis), (), 0, length) for axis, length in enumerate(array.shape)]
        where[longest] = (where[longest] + shift) % array.shape[longest]
        spots.append(tuple(where))
    return array.at[spots[0]].set(smallest).at[spots[1]].set(high)


def levels(key, extent, cuts, smallest, high):
    def one(position, shards_of):
        steps = jax.random.uniform(jax.random.fold_in(jax.random.fold_in(key, 6), position), (shards_of,), jnp.float32, smallest / len(cuts), high / len(cuts))
        return jnp.repeat(jnp.exp(steps), extent[position] // shards_of).reshape((-1,) + (1,) * (len(extent) - position - 1))

    gain = one(*cuts[0])
    for cut in cuts[1:]:
        gain = gain * one(*cut)
    return gain


def bell_draw(own_key, extent, scale, most, shards=(), kind=jnp.bfloat16):
    gain = levels(own_key, extent, shards, -0.22, 0.18) if shards else 1.0
    values = jax.random.normal(own_key, extent, jnp.float32) * scale * gain
    return jnp.minimum(jnp.maximum(values, -most), most).astype(kind)


def setup_inputs(seed: int = 0) -> dict:
    splits = jax.random.split(jax.random.key(seed), 7)
    lambda_cd = bell_draw(splits[0], (IJ, NC, V), 1.0, 6.0, ((0, 16), (1, 16)))
    integrals = bell_draw(splits[1], (NC, V, AB), (NC * V) ** -0.5, 0.01171875, ((0, 16), (2, 16)))
    other_terms = bell_draw(splits[2], (IJ, AB), 1.0, 6.0, ((0, 16), (1, 16)))
    hole_energy = jnp.clip(jnp.exp(jax.random.uniform(splits[3], (NOCC,), jnp.float32, math.log(0.3), math.log(3.0))), 0.3, 3.0)
    virtual_energy = jnp.clip(jnp.exp(jax.random.uniform(splits[4], (VW,), jnp.float32, math.log(0.1), math.log(3.0))), 0.1, 3.0)
    pair_orbitals = with_ends(jax.random.randint(splits[5], (IJ, 2), 0, NOCC), jax.random.fold_in(splits[5], 1), 0, NOCC - 1).astype(jnp.int32)
    return dict(lambda_cd=lambda_cd, integrals=integrals, other_terms=other_terms, hole_energy=hole_energy, virtual_energy=virtual_energy, pair_orbitals=pair_orbitals)


def reference(lambda_cd, integrals, other_terms, hole_energy, virtual_energy, pair_orbitals):
    flat_amps = lambda_cd.reshape(IJ, NC * V)
    flat_ints = integrals.reshape(NC * V, VW * VW)
    ladder = jnp.dot(flat_amps, flat_ints, preferred_element_type=jnp.float32).reshape(IJ, VW, VW)
    antisym = ladder - jnp.transpose(ladder, (0, 2, 1))
    pair_hole = hole_energy[pair_orbitals[:, 0]] + hole_energy[pair_orbitals[:, 1]]
    denom = pair_hole[:, None, None] + virtual_energy[None, :, None] + virtual_energy[None, None, :]
    update = -(other_terms.astype(jnp.float32).reshape(IJ, VW, VW) + 0.5 * antisym) / denom
    return update.reshape(IJ, VW * VW)
```

```python
import functools

import jax
import jax.numpy as jnp
from jax import lax
from jax.experimental import pallas as pl
from jax.experimental.pallas import tpu as pltpu
from jax.sharding import PartitionSpec as P

VW = 64
COLS = 256
ROWS = 32
HALF_ROWS = 16
C_HALF = 8
D_MAIN = 896
D_REST = 4
K_MAIN = C_HALF * D_MAIN
K_ALL = K_MAIN + C_HALF * D_REST
MIB = 1024 * 1024

CHIPS = [(y, h) for y in range(4) for h in range(2)]


def p_of(y, h, core):
    return ((y % 4) * 2 + h % 2) * 2 + core % 2


def bulk_shift(value, dy=0, dh=0, dc=0):
    pairs = []
    for y in range(4):
        for h in range(2):
            for core in range(2):
                pairs.append((p_of(y, h, core), p_of(y + dy, h + dh, core + dc)))
    return lax.ppermute(value, "bulk", pairs)


def x_shift(value, dx):
    pairs = [(x * 4 + zl, ((x + dx) % 4) * 4 + zl) for x in range(4) for zl in range(4)]
    return lax.ppermute(value, "occ", pairs)


def z_flip(value, dh, dz):
    pairs = []
    for y in range(4):
        for h in range(2):
            for core in range(2):
                for x in range(4):
                    for zl in range(4):
                        source = p_of(y, h, core) * 16 + x * 4 + zl
                        target = p_of(y, h ^ dh, core) * 16 + x * 4 + (zl ^ dz)
                        pairs.append((source, target))
    return lax.ppermute(value, ("bulk", "occ"), pairs)


def pack_kernel(core_ref, lam_ref, own0, own1, other0, other1):
    core = core_ref[0]
    n = ROWS * 16
    row = lax.broadcasted_iota(jnp.int32, (n, n), 0)
    col = lax.broadcasted_iota(jnp.int32, (n, n), 1)
    half = row // 256
    c = ((half + core) % 2) * C_HALF + (row % 256) // ROWS
    ij = row % ROWS
    perm = jnp.where(col == ij * 16 + c, 1.0, 0.0).astype(jnp.bfloat16)
    lam = lam_ref[...].reshape(n, D_MAIN + D_REST)
    main = jnp.dot(perm, lam[:, :D_MAIN], preferred_element_type=jnp.float32)
    main = main.astype(jnp.bfloat16)
    rest = jnp.dot(perm, lam[:, D_MAIN:], preferred_element_type=jnp.float32)
    rest = rest.astype(jnp.bfloat16)
    width = C_HALF * D_REST
    source = lax.broadcasted_iota(jnp.int32, (D_REST, width), 0)
    place = lax.broadcasted_iota(jnp.int32, (D_REST, width), 1)
    for k, outs in enumerate(((own0, own1), (other0, other1))):
        total = jnp.zeros((ROWS, width), jnp.float32)
        for i in range(C_HALF):
            start = (k * C_HALF + i) * ROWS
            block = main[start : start + ROWS]
            for s, out in enumerate(outs):
                out[:, i * D_MAIN : (i + 1) * D_MAIN] = block[s * 16 : (s + 1) * 16]
            put = jnp.where(place == source + i * D_REST, 1.0, 0.0).astype(jnp.bfloat16)
            total += jnp.dot(
                rest[start : start + ROWS], put, preferred_element_type=jnp.float32
            )
        total = total.astype(jnp.bfloat16)
        for s, out in enumerate(outs):
            out[:, K_MAIN:] = total[s * 16 : (s + 1) * 16]


def pack(core, lam):
    piece = jax.ShapeDtypeStruct((HALF_ROWS, K_ALL), jnp.bfloat16)
    vmem = pl.BlockSpec(memory_space=pltpu.VMEM)
    return pl.pallas_call(
        pack_kernel,
        out_shape=[piece] * 4,
        in_specs=[pl.BlockSpec(memory_space=pltpu.SMEM), vmem],
        out_specs=[vmem] * 4,
        compiler_params=pltpu.CompilerParams(vmem_limit_bytes=40 * MIB),
        cost_estimate=pl.CostEstimate(
            flops=2 * 512 * 512 * 900, bytes_accessed=2 * MIB, transcendentals=0
        ),
    )(core, lam)


def ladder_kernel(*refs):
    pieces = refs[:8]
    io_ref, is_ref, ro_ref, rs_ref, po_ref, ps_ref, held = refs[8:]
    step = pl.program_id(0)

    @pl.when(step == 0)
    def _():
        for i, piece in enumerate(pieces):
            held[i * 16 : (i + 1) * 16] = piece[...]
        rest = held[:, K_MAIN:]
        for r_ref, out in ((ro_ref, po_ref), (rs_ref, ps_ref)):
            out[...] = jnp.dot(rest, r_ref[...], preferred_element_type=jnp.float32)

    lam = held[:, pl.ds(pl.multiple_of(step * D_MAIN, 128), D_MAIN)]
    for i_ref, out in ((io_ref, po_ref), (is_ref, ps_ref)):
        out[...] += jnp.dot(
            lam, i_ref[0, :D_MAIN, :], preferred_element_type=jnp.float32
        )


def ladder(pieces, ints_own, ints_sib, rest_own, rest_sib):
    m = len(pieces) * HALF_ROWS
    d = D_MAIN + D_REST
    whole = lambda *shape: pl.BlockSpec(shape, lambda i: (0,) * len(shape))
    slab = pl.BlockSpec((1, d, COLS), lambda i: (i, 0, 0))
    out = jax.ShapeDtypeStruct((m, COLS), jnp.float32)
    return pl.pallas_call(
        ladder_kernel,
        grid=(C_HALF,),
        out_shape=[out, out],
        in_specs=[whole(HALF_ROWS, K_ALL)] * 8
        + [slab, slab]
        + [whole(C_HALF * D_REST, COLS)] * 2,
        out_specs=[whole(m, COLS)] * 2,
        scratch_shapes=[pltpu.VMEM((m, K_ALL), jnp.bfloat16)],
        compiler_params=pltpu.CompilerParams(vmem_limit_bytes=32 * MIB),
        cost_estimate=pl.CostEstimate(
            flops=2 * m * K_ALL * 2 * COLS,
            bytes_accessed=2 * K_ALL * (m + 2 * COLS),
            transcendentals=0,
        ),
    )(*pieces, ints_own, ints_sib, rest_own, rest_sib)


def final_kernel(place_ref, t_ref, mine_ref, other_ref, hole_ref, virt_ref, pairs_ref, out_ref):
    y, h, core = place_ref[0], place_ref[1], place_ref[2]
    p = p_of(y, h, core)
    row = lax.broadcasted_iota(jnp.int32, (COLS, COLS), 0)
    col = lax.broadcasted_iota(jnp.int32, (COLS, COLS), 1)
    same_a = row % VW == p * 4 + col // VW
    swapped = jnp.zeros((ROWS, COLS), jnp.float32)
    for sy in range(4):
        for dh in range(2):
            for dc in range(2):
                source = (((y + sy) % 4) * 2 + (h + dh) % 2) * 2 + (core + dc) % 2
                pick = jnp.where(same_a & (col % VW == source * 4 + row // VW), 1.0, 0.0)
                swapped += jnp.dot(
                    t_ref[dc, sy, dh],
                    pick,
                    precision=lax.Precision.HIGHEST,
                    preferred_element_type=jnp.float32,
                )
    orbital = lax.broadcasted_iota(jnp.int32, (ROWS, 60), 1)
    holes = jnp.zeros((ROWS, 1), jnp.float32)
    for k in range(2):
        hit = pairs_ref[:, k : k + 1] == orbital
        holes += jnp.sum(jnp.where(hit, hole_ref[...], 0.0), axis=1, keepdims=True)
    denom = holes + virt_ref[...]
    antisym = mine_ref[...] - swapped
    out_ref[...] = -(other_ref[...].astype(jnp.float32) + 0.5 * antisym) / denom


def final(place, t, mine, other_terms, hole, virt, pairs):
    vmem = pl.BlockSpec(memory_space=pltpu.VMEM)
    return pl.pallas_call(
        final_kernel,
        out_shape=jax.ShapeDtypeStruct((ROWS, COLS), jnp.float32),
        in_specs=[pl.BlockSpec(memory_space=pltpu.SMEM)] + [vmem] * 6,
        out_specs=vmem,
        compiler_params=pltpu.CompilerParams(vmem_limit_bytes=32 * MIB),
    )(place, t, mine, other_terms, hole, virt, pairs)


def gather_chips(own):
    left = bulk_shift(own, dy=1)
    right = bulk_shift(own, dy=-1)
    across = bulk_shift(own, dh=1)
    far = bulk_shift(left, dy=1)
    across_left = bulk_shift(across, dy=1)
    across_right = bulk_shift(across, dy=-1)
    across_far = bulk_shift(across_right, dy=-1)
    return [own, across, right, across_right, far, across_far, left, across_left]


def local(lambda_cd, integrals, other_terms, hole_energy, virtual_energy, pair_orbitals):
    p = lax.axis_index("bulk")
    q = lax.axis_index("occ")
    y, h, core = p // 4, (p // 2) % 2, p % 2
    x, zl = q // 4, q % 4

    own0, own1, other0, other1 = pack(core.reshape(1).astype(jnp.int32), lambda_cd)
    sib0 = bulk_shift(other0, dc=1)
    sib1 = bulk_shift(other1, dc=1)

    ints_own = lax.dynamic_slice_in_dim(integrals, core * C_HALF, C_HALF, axis=0)
    ints_other = lax.dynamic_slice_in_dim(integrals, (1 - core) * C_HALF, C_HALF, axis=0)
    ints_sib = bulk_shift(ints_other, dc=1)
    rest_own = ints_own[:, D_MAIN:, :].reshape(C_HALF * D_REST, COLS)
    rest_sib = ints_sib[:, D_MAIN:, :].reshape(C_HALF * D_REST, COLS)

    mine, sent = [], []
    for piece in (own0, sib0, own1, sib1):
        po, ps = ladder(gather_chips(piece), ints_own, ints_sib, rest_own, rest_sib)
        mine.append(po)
        sent.append(bulk_shift(ps, dc=1))
    shape = (4, 2, HALF_ROWS, COLS)
    totals = [(mine[i] + sent[i ^ 1]).reshape(shape) for i in range(4)]
    total = jnp.stack(
        [
            jnp.concatenate([totals[0], totals[2]], axis=2),
            jnp.concatenate([totals[1], totals[3]], axis=2),
        ],
        axis=2,
    )
    by_x = [
        lax.dynamic_index_in_dim(total, (x + j - y) % 4, axis=0, keepdims=False)
        for j in range(4)
    ]
    rows_x = by_x[0]
    for j in range(1, 4):
        rows_x = rows_x + x_shift(by_x[j], j)
    by_z = []
    for j in range(4):
        target = zl ^ j
        one = lax.dynamic_index_in_dim(rows_x, (target // 2) ^ h, axis=0, keepdims=False)
        by_z.append(
            lax.dynamic_index_in_dim(one, (target % 2) ^ core, axis=0, keepdims=False)
        )
    here = by_z[0]
    there = z_flip(by_z[0], 1, 0)
    for j in range(1, 4):
        here = here + z_flip(by_z[j], 0, j)
        there = there + z_flip(by_z[j], 1, j)
    both = jnp.stack([here, there])
    by_y = [both] + [bulk_shift(both, dy=-s) for s in range(1, 4)]
    by_y = jnp.stack(by_y)
    all_t = jnp.stack([by_y, bulk_shift(by_y, dc=1)])

    own_virtual = lax.dynamic_slice_in_dim(virtual_energy, p * 4, 4)
    virt = (own_virtual[:, None] + virtual_energy[None, :]).reshape(1, COLS)
    place = jnp.stack([y, h, core]).astype(jnp.int32)
    return final(
        place, all_t, here, other_terms, hole_energy.reshape(1, -1), virt, pair_orbitals
    )


def solution(mesh):
    placed = (
        P("bulk", "occ", None),
        P("occ", None, "bulk"),
        P("occ", "bulk"),
        P(),
        P(),
        P("occ", None),
    )
    return jax.shard_map(
        local, mesh=mesh, in_specs=placed, out_specs=P("occ", "bulk"), check_vma=False
    )
```

```python
import functools

import jax
import jax.numpy as jnp
from jax import lax
from jax.experimental import pallas as pl
from jax.experimental.pallas import tpu as pltpu
from jax.sharding import PartitionSpec as P

VW = 64
COLS = 256
ROWS = 32
C_HALF = 8
D = 900
K_ALL = C_HALF * D
MIB = 1024 * 1024
COSTS = (10, 10, 10, 10, 10, 10, 10, 10)


def p_of(y, h, core):
    return ((y % 4) * 2 + h % 2) * 2 + core % 2


def bulk_shift(name, value, dy=0, dh=0, dc=0):
    pairs = []
    for y in range(4):
        for h in range(2):
            for core in range(2):
                pairs.append((p_of(y, h, core), p_of(y + dy, h + dh, core + dc)))
    with jax.named_scope(name):
        return lax.ppermute(value, "bulk", pairs)


def after(value, *others):
    return lax.optimization_barrier((value,) + others)[0]


def pack_kernel(core_ref, lam_ref, own_ref, other_ref):
    core = core_ref[0]
    n = ROWS * 16
    row = lax.broadcasted_iota(jnp.int32, (n, n), 0)
    col = lax.broadcasted_iota(jnp.int32, (n, n), 1)
    c = ((row // 256 + core) % 2) * C_HALF + (row % 256) // ROWS
    perm = jnp.where(col == (row % ROWS) * 16 + c, 1.0, 0.0).astype(jnp.bfloat16)
    lam = lam_ref[...].reshape(n, D)
    full = D // 128 * 128
    main = jnp.dot(perm, lam[:, :full], preferred_element_type=jnp.float32)
    main = main.astype(jnp.bfloat16)
    rest = jnp.dot(perm, lam[:, full:], preferred_element_type=jnp.float32)
    rest = rest.astype(jnp.bfloat16)
    source = lax.broadcasted_iota(jnp.int32, (1024, 1024), 0)
    goal = lax.broadcasted_iota(jnp.int32, (1024, 1024), 1)
    weave = jnp.where(goal == (source % 128) * C_HALF + source // 128, 1.0, 0.0)
    weave = weave.astype(jnp.bfloat16)
    tail = D - full
    source = lax.broadcasted_iota(jnp.int32, (tail, tail * C_HALF), 0)
    goal = lax.broadcasted_iota(jnp.int32, (tail, tail * C_HALF), 1)
    for k, out in enumerate((own_ref, other_ref)):
        first = k * 256
        blocks = [
            jnp.concatenate(
                [
                    main[first + i * ROWS : first + (i + 1) * ROWS, j * 128 : (j + 1) * 128]
                    for i in range(C_HALF)
                ],
                axis=1,
            )
            for j in range(full // 128)
        ]
        woven = jnp.dot(
            jnp.concatenate(blocks, axis=0), weave, preferred_element_type=jnp.float32
        ).astype(jnp.bfloat16)
        for j in range(full // 128):
            out[:, j * 1024 : (j + 1) * 1024] = woven[j * ROWS : (j + 1) * ROWS]
        total = jnp.zeros((ROWS, tail * C_HALF), jnp.float32)
        for i in range(C_HALF):
            put = jnp.where(goal == source * C_HALF + i, 1.0, 0.0).astype(jnp.bfloat16)
            total += jnp.dot(
                rest[first + i * ROWS : first + (i + 1) * ROWS],
                put,
                preferred_element_type=jnp.float32,
            )
        out[:, full * C_HALF :] = total.astype(jnp.bfloat16)


def pack(core, lam):
    piece = jax.ShapeDtypeStruct((ROWS, K_ALL), jnp.bfloat16)
    vmem = pl.BlockSpec(memory_space=pltpu.VMEM)
    return pl.pallas_call(
        pack_kernel,
        out_shape=[piece] * 2,
        in_specs=[pl.BlockSpec(memory_space=pltpu.SMEM), vmem],
        out_specs=[vmem] * 2,
        compiler_params=pltpu.CompilerParams(vmem_limit_bytes=40 * MIB),
        cost_estimate=pl.CostEstimate(
            flops=2 * 512 * 512 * 900, bytes_accessed=2 * MIB, transcendentals=0
        ),
    )(core, lam)


def stage_kernel(in_ref, out_ref):
    pass


def stage(token, *others, cost=10):
    place = pl.BlockSpec(memory_space=pl.ANY)
    return pl.pallas_call(
        stage_kernel,
        out_shape=jax.ShapeDtypeStruct((8, 128), jnp.float32),
        in_specs=[place],
        out_specs=place,
        input_output_aliases={0: 0},
        cost_estimate=pl.CostEstimate(
            flops=cost * 1_000_000_000, bytes_accessed=8192, transcendentals=0
        ),
    )(after(token, *others))


def ladder_kernel(*refs):
    pieces = refs[:-4]
    io_ref, is_ref, po_ref, ps_ref = refs[-4:]
    own, sib = 0.0, 0.0
    for start in range(0, K_ALL, 1024):
        part = slice(start, min(start + 1024, K_ALL))
        lam = jnp.concatenate([piece[:, part] for piece in pieces], axis=0)
        own += jnp.dot(lam, io_ref[part, :], preferred_element_type=jnp.float32)
        sib += jnp.dot(lam, is_ref[part, :], preferred_element_type=jnp.float32)
    po_ref[...] = own
    ps_ref[...] = sib


def ladder(pieces, ints_own, ints_sib):
    m = sum(piece.shape[0] for piece in pieces)
    vmem = pl.BlockSpec(memory_space=pltpu.VMEM)
    out = jax.ShapeDtypeStruct((m, COLS), jnp.float32)
    return pl.pallas_call(
        ladder_kernel,
        out_shape=[out, out],
        in_specs=[vmem] * (len(pieces) + 2),
        out_specs=[vmem] * 2,
        compiler_params=pltpu.CompilerParams(vmem_limit_bytes=40 * MIB),
        cost_estimate=pl.CostEstimate(
            flops=2 * m * K_ALL * 2 * COLS,
            bytes_accessed=2 * K_ALL * (m + 2 * COLS),
            transcendentals=0,
        ),
    )(*pieces, ints_own, ints_sib)


def combine_kernel(spots, place_ref, *refs):
    y, h, core = place_ref[0], place_ref[1], place_ref[2]
    count = len(refs) // 2
    mine, theirs, out_ref = refs[:count], refs[count:-1], refs[-1]
    for (i, sh, sy), (k, row) in spots.items():
        other_k, other_row = spots[1 - i, sh, sy]
        zl = ((h + sh) % 2) * 2 + (core + i) % 2
        out_ref[(y + sy) % 4, zl] = (
            mine[k][row : row + ROWS, :] + theirs[other_k][other_row : other_row + ROWS, :]
        )


def combine(spots, place, mine, theirs):
    vmem = pl.BlockSpec(memory_space=pltpu.VMEM)
    return pl.pallas_call(
        functools.partial(combine_kernel, spots),
        out_shape=jax.ShapeDtypeStruct((4, 4, ROWS, COLS), jnp.float32),
        in_specs=[pl.BlockSpec(memory_space=pltpu.SMEM)] + [vmem] * (2 * len(mine)),
        out_specs=vmem,
        compiler_params=pltpu.CompilerParams(vmem_limit_bytes=16 * MIB),
    )(place, *mine, *theirs)


def spread_kernel(place_ref, t_ref, here_ref, out_ref):
    h = place_ref[1]
    parts = []
    for dh in range(2):
        first = ((h + dh) % 2) * 4
        parts.append(t_ref[first] + t_ref[first + 1] + t_ref[first + 2] + t_ref[first + 3])
    here_ref[...] = parts[0]
    both = jnp.concatenate(parts + [jnp.zeros((2 * ROWS, COLS), jnp.float32)], axis=0)
    row = lax.broadcasted_iota(jnp.int32, (128, COLS), 0)
    col = lax.broadcasted_iota(jnp.int32, (128, COLS), 1)
    target = ((row // 32) * 2 + h) * 2 + (row // 16) % 2
    want = ((row // 4) % 4) * VW + target * 4 + row % 4
    pick = jnp.where(col == want, 1.0, 0.0)
    out_ref[...] = lax.dot_general(
        pick,
        both,
        (((1,), (1,)), ((), ())),
        precision=lax.Precision.HIGHEST,
        preferred_element_type=jnp.float32,
    )


def spread(place, t):
    vmem = pl.BlockSpec(memory_space=pltpu.VMEM)
    return pl.pallas_call(
        spread_kernel,
        out_shape=[
            jax.ShapeDtypeStruct((ROWS, COLS), jnp.float32),
            jax.ShapeDtypeStruct((128, 128), jnp.float32),
        ],
        in_specs=[pl.BlockSpec(memory_space=pltpu.SMEM), vmem],
        out_specs=[vmem] * 2,
        compiler_params=pltpu.CompilerParams(vmem_limit_bytes=16 * MIB),
    )(place, t)


def final_kernel(
    place_ref, t_ref, mine_ref, other_ref, hole_ref, virt_ref, pairs_ref, token_ref, out_ref
):
    h = place_ref[1]
    row = lax.broadcasted_iota(jnp.int32, (128, COLS), 0)
    col = lax.broadcasted_iota(jnp.int32, (128, COLS), 1)
    swapped = jnp.zeros((ROWS, COLS), jnp.float32)
    t = t_ref[...].T
    for dh in range(2):
        source = ((row // 32) * 2 + (h + dh) % 2) * 2 + (row // 16) % 2
        goal = (row % 4) * VW + source * 4 + (row // 4) % 4
        put = jnp.where(col == goal, 1.0, 0.0)
        swapped += jnp.dot(
            t[dh * ROWS : (dh + 1) * ROWS],
            put,
            precision=lax.Precision.HIGHEST,
            preferred_element_type=jnp.float32,
        )
    orbital = lax.broadcasted_iota(jnp.int32, (ROWS, 60), 1)
    holes = jnp.zeros((ROWS, 1), jnp.float32)
    for k in range(2):
        hit = pairs_ref[:, k : k + 1] == orbital
        holes += jnp.sum(jnp.where(hit, hole_ref[...], 0.0), axis=1, keepdims=True)
    denom = holes + virt_ref[...]
    antisym = mine_ref[...] - swapped
    out_ref[...] = -(other_ref[...].astype(jnp.float32) + 0.5 * antisym) / denom


def final(place, t, mine, other_terms, hole, virt, pairs, token):
    vmem = pl.BlockSpec(memory_space=pltpu.VMEM)
    return pl.pallas_call(
        final_kernel,
        out_shape=jax.ShapeDtypeStruct((ROWS, COLS), jnp.float32),
        in_specs=[pl.BlockSpec(memory_space=pltpu.SMEM)] + [vmem] * 7,
        out_specs=vmem,
        compiler_params=pltpu.CompilerParams(vmem_limit_bytes=32 * MIB),
    )(place, t, mine, other_terms, hole, virt, pairs, token)


def group(kind):
    groups = {}
    for p in range(16):
        for q in range(16):
            spot = dict(y=p // 4, h=p // 2 % 2, c=p % 2, x=q // 4, z=q % 4)
            key = tuple(spot[name] for name in "yhcxz" if name not in kind)
            groups.setdefault(key, []).append(p * 16 + q)
    return list(groups.values())


def exchange(value, kind):
    return lax.all_to_all(
        value, ("bulk", "occ"), 0, 0, axis_index_groups=group(kind), tiled=True
    )


def local(lambda_cd, integrals, other_terms, hole_energy, virtual_energy, pair_orbitals):
    p = lax.axis_index("bulk")
    y, h, core = p // 4, (p // 2) % 2, p % 2
    place = jnp.stack([y, h, core]).astype(jnp.int32)

    own, other = pack(core.reshape(1).astype(jnp.int32), lambda_cd)
    shift = bulk_shift
    g = jnp.zeros((8, 128), jnp.float32)
    z0 = shift("z0", own, dh=1)
    sib = shift("sib", other, dc=1)
    r0 = shift("r0", own, dy=-1)
    l0 = shift("l0", own, dy=1)
    g = stage(g, sib, cost=COSTS[0])
    l1 = shift("l1", after(sib, g), dy=1)
    r1 = shift("r1", after(sib, g), dy=-1)
    ints = jnp.transpose(after(integrals, g), (1, 0, 2))
    ints_other = lax.dynamic_slice_in_dim(ints, (1 - core) * C_HALF, C_HALF, axis=1)
    ints_sib = shift("ints", ints_other, dc=1).reshape(K_ALL, COLS)
    g = stage(g, ints_other, cost=COSTS[1])
    z1 = shift("z1", after(sib, g), dh=1)
    g = stage(g, r0, l0, cost=COSTS[2])
    f0 = shift("f0", after(r0, g), dy=-1)
    g = stage(g, r1, l1, cost=COSTS[3])
    f1 = shift("f1", after(l1, g), dy=1)
    g = stage(g, z0, cost=COSTS[4])
    zr0 = shift("zr0", after(z0, g), dy=-1)
    zl0 = shift("zl0", after(z0, g), dy=1)
    ints = jnp.transpose(after(integrals, g), (1, 0, 2))
    ints_own = lax.dynamic_slice_in_dim(ints, core * C_HALF, C_HALF, axis=1)
    ints_own = ints_own.reshape(K_ALL, COLS)
    g = stage(g, z1, f0, f1, cost=COSTS[5])
    zr1 = shift("zr1", after(z1, g), dy=-1)
    zl1 = shift("zl1", after(z1, g), dy=1)
    g = stage(g, zr0, zl0, ints_own, cost=COSTS[6])
    zf0 = shift("zf0", after(zl0, g), dy=1)
    g = stage(g, zr1, cost=COSTS[7])
    zf1 = shift("zf1", after(zr1, g), dy=-1)

    near = {(0, 0, 0): own, (0, 0, 1): r0, (0, 0, 2): f0, (0, 0, 3): l0}
    near |= {(1, 0, 0): sib, (1, 0, 1): r1, (1, 0, 2): f1, (1, 0, 3): l1}
    far = {(0, 1, 0): z0, (0, 1, 1): zr0, (0, 1, 2): zf0, (0, 1, 3): zl0}
    far |= {(1, 1, 0): z1, (1, 1, 1): zr1, (1, 1, 2): zf1, (1, 1, 3): zl1}
    spots, mine, theirs = {}, [], []
    for k, pieces in enumerate((near, far)):
        for n, key in enumerate(pieces):
            spots[key] = (k, n * ROWS)
        po, ps = ladder(tuple(pieces.values()), ints_own, ints_sib)
        mine.append(po)
        theirs.append(shift("t%d" % k, ps, dc=1))
    by_x = combine(spots, place, mine, theirs)
    rows_x = jnp.sum(exchange(by_x, "x"), axis=0)
    by_z = exchange(jnp.concatenate([rows_x, rows_x], axis=0), "hz")
    here, mixed = spread(place, by_z)
    swapped = exchange(mixed.reshape(8, 16, 128), "yc").reshape(128, 128)

    own_virtual = lax.dynamic_slice_in_dim(virtual_energy, p * 4, 4)
    virt = (own_virtual[:, None] + virtual_energy[None, :]).reshape(1, COLS)
    return final(
        place, swapped, here, other_terms, hole_energy.reshape(1, -1), virt, pair_orbitals, g
    )


def solution(mesh):
    placed = (
        P("bulk", "occ", None),
        P("occ", None, "bulk"),
        P("occ", "bulk"),
        P(),
        P(),
        P("occ", None),
    )
    return jax.shard_map(
        local, mesh=mesh, in_specs=placed, out_specs=P("occ", "bulk"), check_vma=False
    )
```

```python
import functools

import jax
import jax.numpy as jnp
from jax import lax
from jax.experimental import pallas as pl
from jax.experimental.pallas import tpu as pltpu
from jax.sharding import PartitionSpec as P

VW = 64
COLS = 256
ROWS = 32
HALF = 16
C_HALF = 8
D = 900
K_ALL = C_HALF * D
MIB = 1024 * 1024
COSTS = (10, 10, 10, 10, 10, 10, 10, 10)


def p_of(y, h, core):
    return ((y % 4) * 2 + h % 2) * 2 + core % 2


def here():
    p = lax.axis_index("bulk")
    return p // 4, (p // 2) % 2, p % 2


def bulk_shift(name, value, dy=0, dh=0, dc=0):
    pairs = []
    for y in range(4):
        for h in range(2):
            for core in range(2):
                pairs.append((p_of(y, h, core), p_of(y + dy, h + dh, core + dc)))
    with jax.named_scope(name):
        return lax.ppermute(value, "bulk", pairs)


def after(value, *others):
    return lax.optimization_barrier((value,) + others)[0]


def pack_kernel(lam_ref, own_ref, other_ref, token_ref):
    _, _, core = here()
    token_ref[...] = jnp.zeros_like(token_ref)
    n = ROWS * 16
    row = lax.broadcasted_iota(jnp.int32, (n, n), 0)
    col = lax.broadcasted_iota(jnp.int32, (n, n), 1)
    c = ((row // 256 + core) % 2) * C_HALF + (row % 256) // ROWS
    perm = jnp.where(col == (row % ROWS) * 16 + c, 1.0, 0.0).astype(jnp.bfloat16)
    lam = lam_ref[...].reshape(n, D)
    full = D // 128 * 128
    main = jnp.dot(perm, lam[:, :full], preferred_element_type=jnp.float32)
    main = main.astype(jnp.bfloat16)
    rest = jnp.dot(perm, lam[:, full:], preferred_element_type=jnp.float32)
    rest = rest.astype(jnp.bfloat16)
    source = lax.broadcasted_iota(jnp.int32, (1024, 1024), 0)
    goal = lax.broadcasted_iota(jnp.int32, (1024, 1024), 1)
    weave = jnp.where(goal == (source % 128) * C_HALF + source // 128, 1.0, 0.0)
    weave = weave.astype(jnp.bfloat16)
    tail = D - full
    source = lax.broadcasted_iota(jnp.int32, (tail, tail * C_HALF), 0)
    goal = lax.broadcasted_iota(jnp.int32, (tail, tail * C_HALF), 1)
    for k, out in enumerate((own_ref, other_ref)):
        first = k * 256
        blocks = [
            jnp.concatenate(
                [
                    main[first + i * ROWS : first + (i + 1) * ROWS, j * 128 : (j + 1) * 128]
                    for i in range(C_HALF)
                ],
                axis=1,
            )
            for j in range(full // 128)
        ]
        woven = jnp.dot(
            jnp.concatenate(blocks, axis=0), weave, preferred_element_type=jnp.float32
        ).astype(jnp.bfloat16)
        for j in range(full // 128):
            out[:, j * 1024 : (j + 1) * 1024] = woven[j * ROWS : (j + 1) * ROWS]
        total = jnp.zeros((ROWS, tail * C_HALF), jnp.float32)
        for i in range(C_HALF):
            put = jnp.where(goal == source * C_HALF + i, 1.0, 0.0).astype(jnp.bfloat16)
            total += jnp.dot(
                rest[first + i * ROWS : first + (i + 1) * ROWS],
                put,
                preferred_element_type=jnp.float32,
            )
        out[:, full * C_HALF :] = total.astype(jnp.bfloat16)


def pack(lam):
    piece = jax.ShapeDtypeStruct((ROWS, K_ALL), jnp.bfloat16)
    vmem = pl.BlockSpec(memory_space=pltpu.VMEM)
    return pl.pallas_call(
        pack_kernel,
        out_shape=[piece, piece, jax.ShapeDtypeStruct((8, 128), jnp.float32)],
        in_specs=[vmem],
        out_specs=[vmem] * 3,
        compiler_params=pltpu.CompilerParams(vmem_limit_bytes=24 * MIB),
        cost_estimate=pl.CostEstimate(
            flops=2 * 512 * 512 * 900, bytes_accessed=2 * MIB, transcendentals=0
        ),
    )(lam)


def stage_kernel(in_ref, out_ref):
    pass


def stage(token, *others, cost=10):
    place = pl.BlockSpec(memory_space=pl.ANY)
    return pl.pallas_call(
        stage_kernel,
        out_shape=jax.ShapeDtypeStruct((8, 128), jnp.float32),
        in_specs=[place],
        out_specs=place,
        input_output_aliases={0: 0},
        compiler_params=pltpu.CompilerParams(vmem_limit_bytes=MIB // 4),
        cost_estimate=pl.CostEstimate(
            flops=cost * 1_000_000_000, bytes_accessed=8192, transcendentals=0
        ),
    )(after(token, *others))


def ladder_kernel(*refs):
    pieces = refs[:-2]
    ints_ref, out_ref = refs[-2:]
    total = 0.0
    for start in range(0, K_ALL, 1024):
        part = slice(start, min(start + 1024, K_ALL))
        lam = jnp.concatenate([piece[:, part] for piece in pieces], axis=0)
        total += jnp.dot(lam, ints_ref[part, :], preferred_element_type=jnp.float32)
    out_ref[...] = total


def ladder(pieces, ints):
    m = sum(piece.shape[0] for piece in pieces)
    vmem = pl.BlockSpec(memory_space=pltpu.VMEM)
    return pl.pallas_call(
        ladder_kernel,
        out_shape=jax.ShapeDtypeStruct((m, COLS), jnp.float32),
        in_specs=[vmem] * (len(pieces) + 1),
        out_specs=vmem,
        compiler_params=pltpu.CompilerParams(vmem_limit_bytes=16 * MIB),
        cost_estimate=pl.CostEstimate(
            flops=2 * m * K_ALL * COLS,
            bytes_accessed=2 * K_ALL * (m + COLS),
            transcendentals=0,
        ),
    )(*pieces, ints)


def combine_kernel(spots, *refs):
    y, h, core = here()
    count = len(refs) // 2
    mine, theirs, out_ref = refs[:count], refs[count:-1], refs[-1]
    for (i, sh, sy), (k, row) in spots.items():
        other_k, other_row = spots[1 - i, sh, sy]
        zl = ((h + sh) % 2) * 2 + (core + i) % 2
        out_ref[(y + sy) % 4, zl] = (
            mine[k][row : row + ROWS, :] + theirs[other_k][other_row : other_row + ROWS, :]
        )


def combine(spots, mine, theirs):
    vmem = pl.BlockSpec(memory_space=pltpu.VMEM)
    return pl.pallas_call(
        functools.partial(combine_kernel, spots),
        out_shape=jax.ShapeDtypeStruct((4, 4, ROWS, COLS), jnp.float32),
        in_specs=[vmem] * (2 * len(mine)),
        out_specs=vmem,
        compiler_params=pltpu.CompilerParams(vmem_limit_bytes=8 * MIB),
    )(*mine, *theirs)


def spread_kernel(t_ref, here_ref, out_ref):
    _, h, _ = here()
    parts = []
    for dh in range(2):
        first = ((h + dh) % 2) * 4
        parts.append(t_ref[first] + t_ref[first + 1] + t_ref[first + 2] + t_ref[first + 3])
    here_ref[...] = parts[0]
    both = jnp.concatenate(parts + [jnp.zeros((2 * ROWS, COLS), jnp.float32)], axis=0)
    row = lax.broadcasted_iota(jnp.int32, (128, COLS), 0)
    col = lax.broadcasted_iota(jnp.int32, (128, COLS), 1)
    target = ((row // 32) * 2 + h) * 2 + (row // 16) % 2
    want = ((row // 4) % 4) * VW + target * 4 + row % 4
    pick = jnp.where(col == want, 1.0, 0.0)
    out_ref[...] = lax.dot_general(
        pick,
        both,
        (((1,), (1,)), ((), ())),
        precision=lax.Precision.HIGHEST,
        preferred_element_type=jnp.float32,
    )


def spread(t):
    vmem = pl.BlockSpec(memory_space=pltpu.VMEM)
    return pl.pallas_call(
        spread_kernel,
        out_shape=[
            jax.ShapeDtypeStruct((ROWS, COLS), jnp.float32),
            jax.ShapeDtypeStruct((128, 128), jnp.float32),
        ],
        in_specs=[vmem],
        out_specs=[vmem] * 2,
        compiler_params=pltpu.CompilerParams(vmem_limit_bytes=8 * MIB),
    )(t)


def final_kernel(t_ref, mine_ref, other_ref, hole_ref, virt_ref, pairs_ref, token_ref, out_ref):
    y, h, core = here()
    exact = dict(precision=lax.Precision.HIGHEST, preferred_element_type=jnp.float32)
    row = lax.broadcasted_iota(jnp.int32, (128, COLS), 0)
    col = lax.broadcasted_iota(jnp.int32, (128, COLS), 1)
    swapped = jnp.zeros((ROWS, COLS), jnp.float32)
    t = t_ref[...].T
    for dh in range(2):
        source = ((row // 32) * 2 + (h + dh) % 2) * 2 + (row // 16) % 2
        goal = (row % 4) * VW + source * 4 + (row // 4) % 4
        put = jnp.where(col == goal, 1.0, 0.0)
        swapped += jnp.dot(t[dh * ROWS : (dh + 1) * ROWS], put, **exact)
    own_a = ((y * 2 + h) * 2 + core) * 4 + col[:VW] // VW
    pick_a = jnp.where(row[:VW] == own_a, 1.0, 0.0)
    pick_b = jnp.where(row[:VW] == col[:VW] % VW, 1.0, 0.0)
    virtual = jnp.broadcast_to(virt_ref[...], (8, VW))
    virt_a = jnp.dot(virtual, pick_a, **exact)[:1]
    virt_b = jnp.dot(virtual, pick_b, **exact)[:1]
    count = hole_ref.shape[1]
    orbital = lax.broadcasted_iota(jnp.int32, (count, ROWS), 0)
    hole = jnp.broadcast_to(hole_ref[...], (8, count))
    diagonal = lax.broadcasted_iota(jnp.int32, (ROWS, ROWS), 0) == lax.broadcasted_iota(
        jnp.int32, (ROWS, ROWS), 1
    )
    holes = jnp.zeros((ROWS, 1), jnp.float32)
    for k in range(2):
        pick = jnp.where(orbital == pairs_ref[k : k + 1, :], 1.0, 0.0)
        energy = jnp.dot(hole, pick, **exact)[:1]
        holes += jnp.sum(jnp.where(diagonal, energy, 0.0), axis=1, keepdims=True)
    denom = holes + virt_a + virt_b
    antisym = mine_ref[...] - swapped
    out_ref[...] = -(other_ref[...].astype(jnp.float32) + 0.5 * antisym) / denom


def final(t, mine, other_terms, hole, virt, pairs, token):
    vmem = pl.BlockSpec(memory_space=pltpu.VMEM)
    return pl.pallas_call(
        final_kernel,
        out_shape=jax.ShapeDtypeStruct((ROWS, COLS), jnp.float32),
        in_specs=[vmem] * 6 + [pl.BlockSpec(memory_space=pl.ANY)],
        out_specs=vmem,
        compiler_params=pltpu.CompilerParams(vmem_limit_bytes=8 * MIB),
    )(t, mine, other_terms, hole, virt, pairs, token)


def group(kind):
    groups = {}
    for p in range(16):
        for q in range(16):
            spot = dict(y=p // 4, h=p // 2 % 2, c=p % 2, x=q // 4, z=q % 4)
            key = tuple(spot[name] for name in "yhcxz" if name not in kind)
            groups.setdefault(key, []).append(p * 16 + q)
    return list(groups.values())


def exchange(value, kind):
    return lax.all_to_all(
        value, ("bulk", "occ"), 0, 0, axis_index_groups=group(kind), tiled=True
    )


def local(lambda_cd, integrals, other_terms, hole_energy, virtual_energy, pair_orbitals):
    core = lax.axis_index("bulk") % 2
    own, other, g = pack(lambda_cd)
    shift = bulk_shift
    z0 = shift("z0", own, dh=1)
    sib = shift("sib", other, dc=1)
    r0 = shift("r0", own, dy=-1)
    l0 = shift("l0", own, dy=1)
    g = stage(g, sib, cost=COSTS[0])
    l1 = shift("l1", after(sib, g), dy=1)
    r1 = shift("r1", after(sib, g), dy=-1)
    ints = jnp.transpose(after(integrals, g), (1, 0, 2))
    ints_other = lax.dynamic_slice_in_dim(ints, (1 - core) * C_HALF, C_HALF, axis=1)
    ints_sib = shift("ints", ints_other, dc=1).reshape(K_ALL, COLS)
    g = stage(g, ints_other, cost=COSTS[1])
    z1 = shift("z1", after(sib, g), dh=1)
    g = stage(g, r0, l0, cost=COSTS[2])
    f0 = shift("f0", after(r0, g), dy=-1)
    g = stage(g, r1, l1, cost=COSTS[3])
    f1 = shift("f1", after(l1, g), dy=1)
    g = stage(g, z0, cost=COSTS[4])
    zr0 = shift("zr0", after(z0, g), dy=-1)
    zl0 = shift("zl0", after(z0, g), dy=1)
    ints = jnp.transpose(after(integrals, g), (1, 0, 2))
    ints_own = lax.dynamic_slice_in_dim(ints, core * C_HALF, C_HALF, axis=1)
    ints_own = ints_own.reshape(K_ALL, COLS)
    g = stage(g, z1, f0, f1, cost=COSTS[5])
    zr1 = shift("zr1", after(z1, g), dy=-1)
    zl1 = shift("zl1", after(z1, g), dy=1)
    g = stage(g, zr0, zl0, ints_own, cost=COSTS[6])
    zf0 = shift("zf0", after(zl0, g), dy=1)
    g = stage(g, zr1, cost=COSTS[7])
    zf1 = shift("zf1", after(zr1, g), dy=-1)

    near = {(0, 0, 0): own, (0, 0, 1): r0, (0, 0, 2): f0, (0, 0, 3): l0}
    near |= {(1, 0, 0): sib, (1, 0, 1): r1, (1, 0, 2): f1, (1, 0, 3): l1}
    far = {(0, 1, 0): z0, (0, 1, 1): zr0, (0, 1, 2): zf0, (0, 1, 3): zl0}
    far |= {(1, 1, 0): z1, (1, 1, 1): zr1, (1, 1, 2): zf1, (1, 1, 3): zl1}
    spots, mine, theirs = {}, [], []
    for k, pieces in enumerate((near, far)):
        for n, key in enumerate(pieces):
            spots[key] = (k, n * ROWS)
        pieces = jax.tree.leaves(list(pieces.values()))
        part = ladder(pieces, after(ints_sib, *mine, *theirs))
        theirs.append(shift("t%d" % k, part, dc=1))
        mine.append(ladder(pieces, after(ints_own, part)))
    by_x = combine(spots, mine, theirs)
    rows_x = jnp.sum(exchange(by_x, "x"), axis=0)
    by_z = jnp.broadcast_to(rows_x[None], (2,) + rows_x.shape).reshape(8, ROWS, COLS)
    by_z = exchange(by_z, "hz")
    direct, mixed = spread(by_z)
    swapped = exchange(mixed.reshape(8, 16, 128), "yc").reshape(128, 128)

    return final(
        swapped,
        direct,
        other_terms,
        hole_energy.reshape(1, -1),
        virtual_energy.reshape(1, -1),
        pair_orbitals.T,
        g,
    )


def solution(mesh):
    placed = (
        P("bulk", "occ", None),
        P("occ", None, "bulk"),
        P("occ", "bulk"),
        P(),
        P(),
        P("occ", None),
    )
    return jax.shard_map(
        local, mesh=mesh, in_specs=placed, out_specs=P("occ", "bulk"), check_vma=False
    )
```

```python
import functools

import jax
import jax.numpy as jnp
from jax import lax
from jax.experimental import pallas as pl
from jax.experimental.pallas import tpu as pltpu
from jax.sharding import PartitionSpec as P

VW = 64
COLS = 256
ROWS = 32
HALF = 16
C_HALF = 8
D = 900
K_ALL = C_HALF * D
MIB = 1024 * 1024
COSTS = (10, 10, 10, 10, 10, 10, 10, 10)


def p_of(y, h, core):
    return ((y % 4) * 2 + h % 2) * 2 + core % 2


def here():
    p = lax.axis_index("bulk")
    return p // 4, (p // 2) % 2, p % 2


def bulk_shift(name, value, dy=0, dh=0, dc=0):
    pairs = []
    for y in range(4):
        for h in range(2):
            for core in range(2):
                pairs.append((p_of(y, h, core), p_of(y + dy, h + dh, core + dc)))
    with jax.named_scope(name):
        return lax.ppermute(value, "bulk", pairs)


def after(value, *others):
    return lax.optimization_barrier((value,) + others)[0]


def pack_kernel(lam_ref, own_ref, other_ref, token_ref):
    _, _, core = here()
    token_ref[...] = jnp.zeros_like(token_ref)
    n = ROWS * 16
    row = lax.broadcasted_iota(jnp.int32, (n, n), 0)
    col = lax.broadcasted_iota(jnp.int32, (n, n), 1)
    c = ((row // 256 + core) % 2) * C_HALF + (row % 256) // ROWS
    perm = jnp.where(col == (row % ROWS) * 16 + c, 1.0, 0.0).astype(jnp.bfloat16)
    lam = lam_ref[...].reshape(n, D)
    full = D // 128 * 128
    main = jnp.dot(perm, lam[:, :full], preferred_element_type=jnp.float32)
    main = main.astype(jnp.bfloat16)
    rest = jnp.dot(perm, lam[:, full:], preferred_element_type=jnp.float32)
    rest = rest.astype(jnp.bfloat16)
    source = lax.broadcasted_iota(jnp.int32, (1024, 1024), 0)
    goal = lax.broadcasted_iota(jnp.int32, (1024, 1024), 1)
    weave = jnp.where(goal == (source % 128) * C_HALF + source // 128, 1.0, 0.0)
    weave = weave.astype(jnp.bfloat16)
    tail = D - full
    source = lax.broadcasted_iota(jnp.int32, (tail, tail * C_HALF), 0)
    goal = lax.broadcasted_iota(jnp.int32, (tail, tail * C_HALF), 1)
    for k, out in enumerate((own_ref, other_ref)):
        first = k * 256
        blocks = [
            jnp.concatenate(
                [
                    main[first + i * ROWS : first + (i + 1) * ROWS, j * 128 : (j + 1) * 128]
                    for i in range(C_HALF)
                ],
                axis=1,
            )
            for j in range(full // 128)
        ]
        woven = jnp.dot(
            jnp.concatenate(blocks, axis=0), weave, preferred_element_type=jnp.float32
        ).astype(jnp.bfloat16)
        for j in range(full // 128):
            out[:, j * 1024 : (j + 1) * 1024] = woven[j * ROWS : (j + 1) * ROWS]
        total = jnp.zeros((ROWS, tail * C_HALF), jnp.float32)
        for i in range(C_HALF):
            put = jnp.where(goal == source * C_HALF + i, 1.0, 0.0).astype(jnp.bfloat16)
            total += jnp.dot(
                rest[first + i * ROWS : first + (i + 1) * ROWS],
                put,
                preferred_element_type=jnp.float32,
            )
        out[:, full * C_HALF :] = total.astype(jnp.bfloat16)


def pack(lam):
    piece = jax.ShapeDtypeStruct((ROWS, K_ALL), jnp.bfloat16)
    vmem = pl.BlockSpec(memory_space=pltpu.VMEM)
    return pl.pallas_call(
        pack_kernel,
        out_shape=[piece, piece, jax.ShapeDtypeStruct((8, 128), jnp.float32)],
        in_specs=[vmem],
        out_specs=[vmem] * 3,
        compiler_params=pltpu.CompilerParams(vmem_limit_bytes=24 * MIB),
        cost_estimate=pl.CostEstimate(
            flops=2 * 512 * 512 * 900, bytes_accessed=2 * MIB, transcendentals=0
        ),
    )(lam)


def stage_kernel(in_ref, out_ref):
    pass


def stage(token, *others, cost=10):
    place = pl.BlockSpec(memory_space=pl.ANY)
    return pl.pallas_call(
        stage_kernel,
        out_shape=jax.ShapeDtypeStruct((8, 128), jnp.float32),
        in_specs=[place],
        out_specs=place,
        input_output_aliases={0: 0},
        compiler_params=pltpu.CompilerParams(vmem_limit_bytes=MIB // 4),
        cost_estimate=pl.CostEstimate(
            flops=cost * 1_000_000_000, bytes_accessed=8192, transcendentals=0
        ),
    )(after(token, *others))


def ladder_kernel(*refs):
    pieces = refs[:-2]
    ints_ref, out_ref = refs[-2:]
    total = 0.0
    for start in range(0, K_ALL, 1024):
        part = slice(start, min(start + 1024, K_ALL))
        lam = jnp.concatenate([piece[:, part] for piece in pieces], axis=0)
        total += jnp.dot(lam, ints_ref[part, :], preferred_element_type=jnp.float32)
    out_ref[...] = total


def ladder(pieces, ints):
    m = sum(piece.shape[0] for piece in pieces)
    vmem = pl.BlockSpec(memory_space=pltpu.VMEM)
    return pl.pallas_call(
        ladder_kernel,
        out_shape=jax.ShapeDtypeStruct((m, COLS), jnp.float32),
        in_specs=[vmem] * (len(pieces) + 1),
        out_specs=vmem,
        compiler_params=pltpu.CompilerParams(vmem_limit_bytes=16 * MIB),
        cost_estimate=pl.CostEstimate(
            flops=2 * m * K_ALL * COLS,
            bytes_accessed=2 * K_ALL * (m + COLS),
            transcendentals=0,
        ),
    )(*pieces, ints)


def combine_kernel(spots, *refs):
    y, h, core = here()
    count = len(refs) // 2
    mine, theirs, out_ref = refs[:count], refs[count:-1], refs[-1]
    for (i, sh, sy), (k, row) in spots.items():
        other_k, other_row = spots[1 - i, sh, sy]
        zl = ((h + sh) % 2) * 2 + (core + i) % 2
        out_ref[(y + sy) % 4, zl] = (
            mine[k][row : row + ROWS, :] + theirs[other_k][other_row : other_row + ROWS, :]
        )


def combine(spots, mine, theirs):
    vmem = pl.BlockSpec(memory_space=pltpu.VMEM)
    return pl.pallas_call(
        functools.partial(combine_kernel, spots),
        out_shape=jax.ShapeDtypeStruct((4, 4, ROWS, COLS), jnp.float32),
        in_specs=[vmem] * (2 * len(mine)),
        out_specs=vmem,
        compiler_params=pltpu.CompilerParams(vmem_limit_bytes=8 * MIB),
    )(*mine, *theirs)


def spread_kernel(t_ref, here_ref, out_ref):
    _, h, _ = here()
    parts = []
    for dh in range(2):
        first = ((h + dh) % 2) * 4
        parts.append(t_ref[first] + t_ref[first + 1] + t_ref[first + 2] + t_ref[first + 3])
    here_ref[...] = parts[0]
    both = jnp.concatenate(parts + [jnp.zeros((2 * ROWS, COLS), jnp.float32)], axis=0)
    row = lax.broadcasted_iota(jnp.int32, (128, COLS), 0)
    col = lax.broadcasted_iota(jnp.int32, (128, COLS), 1)
    target = ((row // 32) * 2 + h) * 2 + (row // 16) % 2
    want = ((row // 4) % 4) * VW + target * 4 + row % 4
    pick = jnp.where(col == want, 1.0, 0.0)
    out_ref[...] = lax.dot_general(
        pick,
        both,
        (((1,), (1,)), ((), ())),
        precision=lax.Precision.HIGHEST,
        preferred_element_type=jnp.float32,
    )


def spread(t):
    vmem = pl.BlockSpec(memory_space=pltpu.VMEM)
    return pl.pallas_call(
        spread_kernel,
        out_shape=[
            jax.ShapeDtypeStruct((ROWS, COLS), jnp.float32),
            jax.ShapeDtypeStruct((128, 128), jnp.float32),
        ],
        in_specs=[vmem],
        out_specs=[vmem] * 2,
        compiler_params=pltpu.CompilerParams(vmem_limit_bytes=8 * MIB),
    )(t)


def final_kernel(t_ref, mine_ref, other_ref, hole_ref, virt_ref, pairs_ref, token_ref, out_ref):
    y, h, core = here()
    exact = dict(precision=lax.Precision.HIGHEST, preferred_element_type=jnp.float32)
    row = lax.broadcasted_iota(jnp.int32, (128, COLS), 0)
    col = lax.broadcasted_iota(jnp.int32, (128, COLS), 1)
    swapped = jnp.zeros((ROWS, COLS), jnp.float32)
    t = t_ref[...].T
    for dh in range(2):
        source = ((row // 32) * 2 + (h + dh) % 2) * 2 + (row // 16) % 2
        goal = (row % 4) * VW + source * 4 + (row // 4) % 4
        put = jnp.where(col == goal, 1.0, 0.0)
        swapped += jnp.dot(t[dh * ROWS : (dh + 1) * ROWS], put, **exact)
    own_a = ((y * 2 + h) * 2 + core) * 4 + col[:VW] // VW
    pick_a = jnp.where(row[:VW] == own_a, 1.0, 0.0)
    pick_b = jnp.where(row[:VW] == col[:VW] % VW, 1.0, 0.0)
    virtual = jnp.broadcast_to(virt_ref[...], (8, VW))
    virt_a = jnp.dot(virtual, pick_a, **exact)[:1]
    virt_b = jnp.dot(virtual, pick_b, **exact)[:1]
    count = hole_ref.shape[1]
    orbital = lax.broadcasted_iota(jnp.int32, (count, ROWS), 0)
    hole = jnp.broadcast_to(hole_ref[...], (8, count))
    diagonal = lax.broadcasted_iota(jnp.int32, (ROWS, ROWS), 0) == lax.broadcasted_iota(
        jnp.int32, (ROWS, ROWS), 1
    )
    holes = jnp.zeros((ROWS, 1), jnp.float32)
    for k in range(2):
        pick = jnp.where(orbital == pairs_ref[k : k + 1, :], 1.0, 0.0)
        energy = jnp.dot(hole, pick, **exact)[:1]
        holes += jnp.sum(jnp.where(diagonal, energy, 0.0), axis=1, keepdims=True)
    denom = holes + virt_a + virt_b
    antisym = mine_ref[...] - swapped
    out_ref[...] = -(other_ref[...].astype(jnp.float32) + 0.5 * antisym) / denom


def final(t, mine, other_terms, hole, virt, pairs, token):
    vmem = pl.BlockSpec(memory_space=pltpu.VMEM)
    return pl.pallas_call(
        final_kernel,
        out_shape=jax.ShapeDtypeStruct((ROWS, COLS), jnp.float32),
        in_specs=[vmem] * 6 + [pl.BlockSpec(memory_space=pl.ANY)],
        out_specs=vmem,
        compiler_params=pltpu.CompilerParams(vmem_limit_bytes=8 * MIB),
    )(t, mine, other_terms, hole, virt, pairs, token)


def group(kind):
    groups = {}
    for p in range(16):
        for q in range(16):
            spot = dict(y=p // 4, h=p // 2 % 2, c=p % 2, x=q // 4, z=q % 4)
            key = tuple(spot[name] for name in "yhcxz" if name not in kind)
            groups.setdefault(key, []).append(p * 16 + q)
    return list(groups.values())


def exchange(value, kind):
    return lax.all_to_all(
        value, ("bulk", "occ"), 0, 0, axis_index_groups=group(kind), tiled=True
    )


def local(lambda_cd, integrals, other_terms, hole_energy, virtual_energy, pair_orbitals):
    core = lax.axis_index("bulk") % 2
    shift = bulk_shift
    own, other, g = pack(lambda_cd)
    z0 = shift("z0", own, dh=1)
    r0 = shift("r0", own, dy=-1)
    l0 = shift("l0", own, dy=1)
    sib = shift("sib", other, dc=1)
    g = stage(g, sib, cost=COSTS[0])
    l1 = shift("l1", after(sib, g), dy=1)
    r1 = shift("r1", after(sib, g), dy=-1)
    z1 = shift("z1", after(sib, g), dh=1)
    g = stage(g, r0, l0, cost=COSTS[2])
    f0 = shift("f0", after(r0, g), dy=-1)
    ints = jnp.transpose(after(integrals, g), (1, 0, 2))
    ints_other = lax.dynamic_slice_in_dim(ints, (1 - core) * C_HALF, C_HALF, axis=1)
    ints_sib = shift("ints", ints_other, dc=1).reshape(K_ALL, COLS)
    g = stage(g, r1, l1, cost=COSTS[3])
    f1 = shift("f1", after(l1, g), dy=1)
    g = stage(g, z0, cost=COSTS[4])
    zr0 = shift("zr0", after(z0, g), dy=-1)
    zl0 = shift("zl0", after(z0, g), dy=1)
    g = stage(g, z1, f0, f1, cost=COSTS[5])
    zr1 = shift("zr1", after(z1, g), dy=-1)
    zl1 = shift("zl1", after(z1, g), dy=1)
    g = stage(g, zr0, zl0, cost=COSTS[6])
    zf0 = shift("zf0", after(zl0, g), dy=1)
    ints = jnp.transpose(after(integrals, g), (1, 0, 2))
    ints_own = lax.dynamic_slice_in_dim(ints, core * C_HALF, C_HALF, axis=1)
    ints_own = ints_own.reshape(K_ALL, COLS)
    g = stage(g, zr1, ints_own, cost=COSTS[7])
    zf1 = shift("zf1", after(zr1, g), dy=-1)

    near = {(0, 0, 0): own, (0, 0, 1): r0, (0, 0, 2): f0, (0, 0, 3): l0}
    near |= {(1, 0, 0): sib, (1, 0, 1): r1, (1, 0, 2): f1, (1, 0, 3): l1}
    far = {(0, 1, 0): z0, (0, 1, 1): zr0, (0, 1, 2): zf0, (0, 1, 3): zl0}
    far |= {(1, 1, 0): z1, (1, 1, 1): zr1, (1, 1, 2): zf1, (1, 1, 3): zl1}
    spots, mine, theirs = {}, [], []
    for k, pieces in enumerate((near, far)):
        for n, key in enumerate(pieces):
            spots[key] = (k, n * ROWS)
        pieces = jax.tree.leaves(list(pieces.values()))
        part = ladder(pieces, after(ints_sib, *mine, *theirs))
        theirs.append(shift("t%d" % k, part, dc=1))
        mine.append(ladder(pieces, after(ints_own, part)))
    by_x = combine(spots, mine, theirs)
    rows_x = jnp.sum(exchange(by_x, "x"), axis=0)
    by_z = jnp.broadcast_to(rows_x[None], (2,) + rows_x.shape).reshape(8, ROWS, COLS)
    by_z = exchange(by_z, "hz")
    direct, mixed = spread(by_z)
    swapped = exchange(mixed.reshape(8, 16, 128), "yc").reshape(128, 128)

    return final(
        swapped,
        direct,
        other_terms,
        hole_energy.reshape(1, -1),
        virtual_energy.reshape(1, -1),
        pair_orbitals.T,
        g,
    )


def solution(mesh):
    placed = (
        P("bulk", "occ", None),
        P("occ", None, "bulk"),
        P("occ", "bulk"),
        P(),
        P(),
        P("occ", None),
    )
    return jax.shard_map(
        local, mesh=mesh, in_specs=placed, out_specs=P("occ", "bulk"), check_vma=False
    )
```

```python
import functools

import jax
import jax.numpy as jnp
from jax import lax
from jax.experimental import pallas as pl
from jax.experimental.pallas import tpu as pltpu
from jax.sharding import PartitionSpec as P

VW = 64
COLS = 256
ROWS = 32
HALF = 16
C_HALF = 8
D = 900
K_ALL = C_HALF * D
MIB = 1024 * 1024
COSTS = (10, 10, 10, 10, 10, 10, 10, 10)


def p_of(y, h, core):
    return ((y % 4) * 2 + h % 2) * 2 + core % 2


def here():
    p = lax.axis_index("bulk")
    return p // 4, (p // 2) % 2, p % 2


def bulk_shift(name, value, dy=0, dh=0, dc=0):
    pairs = []
    for y in range(4):
        for h in range(2):
            for core in range(2):
                pairs.append((p_of(y, h, core), p_of(y + dy, h + dh, core + dc)))
    with jax.named_scope(name):
        return lax.ppermute(value, "bulk", pairs)


def after(value, *others):
    return lax.optimization_barrier((value,) + others)[0]


def pack_kernel(lam_ref, own_ref, other_ref, token_ref):
    _, _, core = here()
    token_ref[...] = jnp.zeros_like(token_ref)
    n = ROWS * 16
    full = D // 128 * 128
    lam = jnp.transpose(lam_ref[...].astype(jnp.float32), (1, 0, 2))
    turned = jnp.concatenate([lam[C_HALF:], lam[:C_HALF]], axis=0)
    lam = jnp.where(core == 0, lam, turned).astype(jnp.bfloat16).reshape(n, D)
    main, rest = lam[:, :full], lam[:, full:]
    col = lax.broadcasted_iota(jnp.int32, (1, 1024), 1)
    row = lax.broadcasted_iota(jnp.int32, (1024, 1024), 0)
    weave = jnp.where(row == col % C_HALF * 128 + col // C_HALF, 1.0, 0.0)
    weave = weave.astype(jnp.bfloat16)
    tail = D - full
    source = lax.broadcasted_iota(jnp.int32, (tail, tail * C_HALF), 0)
    goal = lax.broadcasted_iota(jnp.int32, (tail, tail * C_HALF), 1)
    for k, out in enumerate((own_ref, other_ref)):
        first = k * 256
        blocks = [
            jnp.concatenate(
                [
                    main[first + i * ROWS : first + (i + 1) * ROWS, j * 128 : (j + 1) * 128]
                    for i in range(C_HALF)
                ],
                axis=1,
            )
            for j in range(full // 128)
        ]
        woven = jnp.dot(
            jnp.concatenate(blocks, axis=0), weave, preferred_element_type=jnp.float32
        ).astype(jnp.bfloat16)
        for j in range(full // 128):
            out[:, j * 1024 : (j + 1) * 1024] = woven[j * ROWS : (j + 1) * ROWS]
        total = jnp.zeros((ROWS, tail * C_HALF), jnp.float32)
        for i in range(C_HALF):
            put = jnp.where(goal == source * C_HALF + i, 1.0, 0.0).astype(jnp.bfloat16)
            total += jnp.dot(
                rest[first + i * ROWS : first + (i + 1) * ROWS],
                put,
                preferred_element_type=jnp.float32,
            )
        out[:, full * C_HALF :] = total.astype(jnp.bfloat16)


def pack(lam):
    piece = jax.ShapeDtypeStruct((ROWS, K_ALL), jnp.bfloat16)
    vmem = pl.BlockSpec(memory_space=pltpu.VMEM)
    return pl.pallas_call(
        pack_kernel,
        out_shape=[piece, piece, jax.ShapeDtypeStruct((8, 128), jnp.float32)],
        in_specs=[vmem],
        out_specs=[vmem] * 3,
        compiler_params=pltpu.CompilerParams(vmem_limit_bytes=24 * MIB),
        cost_estimate=pl.CostEstimate(
            flops=2 * 512 * 512 * 900, bytes_accessed=2 * MIB, transcendentals=0
        ),
    )(lam)


def stage_kernel(in_ref, out_ref):
    pass


def stage(token, *others, cost=10):
    place = pl.BlockSpec(memory_space=pl.ANY)
    return pl.pallas_call(
        stage_kernel,
        out_shape=jax.ShapeDtypeStruct((8, 128), jnp.float32),
        in_specs=[place],
        out_specs=place,
        input_output_aliases={0: 0},
        compiler_params=pltpu.CompilerParams(vmem_limit_bytes=MIB // 4),
        cost_estimate=pl.CostEstimate(
            flops=cost * 1_000_000_000, bytes_accessed=8192, transcendentals=0
        ),
    )(after(token, *others))


def ladder_kernel(*refs):
    pieces = refs[:-2]
    ints_ref, out_ref = refs[-2:]
    total = 0.0
    for start in range(0, K_ALL, 1024):
        part = slice(start, min(start + 1024, K_ALL))
        lam = jnp.concatenate([piece[:, part] for piece in pieces], axis=0)
        total += jnp.dot(lam, ints_ref[part, :], preferred_element_type=jnp.float32)
    out_ref[...] = total


def ladder(pieces, ints):
    m = sum(piece.shape[0] for piece in pieces)
    vmem = pl.BlockSpec(memory_space=pltpu.VMEM)
    return pl.pallas_call(
        ladder_kernel,
        out_shape=jax.ShapeDtypeStruct((m, COLS), jnp.float32),
        in_specs=[vmem] * (len(pieces) + 1),
        out_specs=vmem,
        compiler_params=pltpu.CompilerParams(vmem_limit_bytes=16 * MIB),
        cost_estimate=pl.CostEstimate(
            flops=2 * m * K_ALL * COLS,
            bytes_accessed=2 * K_ALL * (m + COLS),
            transcendentals=0,
        ),
    )(*pieces, ints)


def combine_kernel(spots, *refs):
    y, h, core = here()
    count = len(refs) // 2
    mine, theirs, out_ref = refs[:count], refs[count:-1], refs[-1]
    for (i, sh, sy), (k, row) in spots.items():
        other_k, other_row = spots[1 - i, sh, sy]
        zl = ((h + sh) % 2) * 2 + (core + i) % 2
        out_ref[(y + sy) % 4, zl] = (
            mine[k][row : row + ROWS, :] + theirs[other_k][other_row : other_row + ROWS, :]
        )


def combine(spots, mine, theirs):
    vmem = pl.BlockSpec(memory_space=pltpu.VMEM)
    return pl.pallas_call(
        functools.partial(combine_kernel, spots),
        out_shape=jax.ShapeDtypeStruct((4, 4, ROWS, COLS), jnp.float32),
        in_specs=[vmem] * (2 * len(mine)),
        out_specs=vmem,
        compiler_params=pltpu.CompilerParams(vmem_limit_bytes=8 * MIB),
    )(*mine, *theirs)


def spread_kernel(t_ref, here_ref, out_ref):
    _, h, _ = here()
    parts = []
    for dh in range(2):
        first = ((h + dh) % 2) * 4
        parts.append(t_ref[first] + t_ref[first + 1] + t_ref[first + 2] + t_ref[first + 3])
    here_ref[...] = parts[0]
    both = jnp.concatenate(parts + [jnp.zeros((2 * ROWS, COLS), jnp.float32)], axis=0)
    row = lax.broadcasted_iota(jnp.int32, (128, COLS), 0)
    col = lax.broadcasted_iota(jnp.int32, (128, COLS), 1)
    target = ((row // 32) * 2 + h) * 2 + (row // 16) % 2
    want = ((row // 4) % 4) * VW + target * 4 + row % 4
    pick = jnp.where(col == want, 1.0, 0.0)
    out_ref[...] = lax.dot_general(
        pick,
        both,
        (((1,), (1,)), ((), ())),
        precision=lax.Precision.HIGHEST,
        preferred_element_type=jnp.float32,
    )


def spread(t):
    vmem = pl.BlockSpec(memory_space=pltpu.VMEM)
    return pl.pallas_call(
        spread_kernel,
        out_shape=[
            jax.ShapeDtypeStruct((ROWS, COLS), jnp.float32),
            jax.ShapeDtypeStruct((128, 128), jnp.float32),
        ],
        in_specs=[vmem],
        out_specs=[vmem] * 2,
        compiler_params=pltpu.CompilerParams(vmem_limit_bytes=8 * MIB),
    )(t)


def denom_kernel(hole_ref, virt_ref, pairs_ref, out_ref):
    y, h, core = here()
    exact = dict(precision=lax.Precision.HIGHEST, preferred_element_type=jnp.float32)
    row = lax.broadcasted_iota(jnp.int32, (VW, COLS), 0)
    col = lax.broadcasted_iota(jnp.int32, (VW, COLS), 1)
    own_a = ((y * 2 + h) * 2 + core) * 4 + col // VW
    pick_a = jnp.where(row == own_a, 1.0, 0.0)
    pick_b = jnp.where(row == col % VW, 1.0, 0.0)
    virtual = jnp.broadcast_to(virt_ref[...], (8, VW))
    virt_a = jnp.dot(virtual, pick_a, **exact)[:1]
    virt_b = jnp.dot(virtual, pick_b, **exact)[:1]
    count = hole_ref.shape[1]
    orbital = lax.broadcasted_iota(jnp.int32, (count, ROWS), 0)
    hole = jnp.broadcast_to(hole_ref[...], (8, count))
    diagonal = lax.broadcasted_iota(jnp.int32, (ROWS, ROWS), 0) == lax.broadcasted_iota(
        jnp.int32, (ROWS, ROWS), 1
    )
    holes = jnp.zeros((ROWS, 1), jnp.float32)
    for k in range(2):
        pick = jnp.where(orbital == pairs_ref[k : k + 1, :], 1.0, 0.0)
        energy = jnp.dot(hole, pick, **exact)[:1]
        holes += jnp.sum(jnp.where(diagonal, energy, 0.0), axis=1, keepdims=True)
    out_ref[...] = holes + virt_a + virt_b


def denominators(hole, virt, pairs):
    vmem = pl.BlockSpec(memory_space=pltpu.VMEM)
    return pl.pallas_call(
        denom_kernel,
        out_shape=jax.ShapeDtypeStruct((ROWS, COLS), jnp.float32),
        in_specs=[vmem] * 3,
        out_specs=vmem,
        compiler_params=pltpu.CompilerParams(vmem_limit_bytes=8 * MIB),
    )(hole, virt, pairs)


def final_kernel(t_ref, mine_ref, other_ref, denom_ref, token_ref, out_ref):
    _, h, _ = here()
    exact = dict(precision=lax.Precision.HIGHEST, preferred_element_type=jnp.float32)
    row = lax.broadcasted_iota(jnp.int32, (128, COLS), 0)
    col = lax.broadcasted_iota(jnp.int32, (128, COLS), 1)
    swapped = jnp.zeros((ROWS, COLS), jnp.float32)
    t = t_ref[...].T
    for dh in range(2):
        source = ((row // 32) * 2 + (h + dh) % 2) * 2 + (row // 16) % 2
        goal = (row % 4) * VW + source * 4 + (row // 4) % 4
        put = jnp.where(col == goal, 1.0, 0.0)
        swapped += jnp.dot(t[dh * ROWS : (dh + 1) * ROWS], put, **exact)
    antisym = mine_ref[...] - swapped
    out_ref[...] = -(other_ref[...].astype(jnp.float32) + 0.5 * antisym) / denom_ref[...]


def final(t, mine, other_terms, denom, token):
    vmem = pl.BlockSpec(memory_space=pltpu.VMEM)
    return pl.pallas_call(
        final_kernel,
        out_shape=jax.ShapeDtypeStruct((ROWS, COLS), jnp.float32),
        in_specs=[vmem] * 4 + [pl.BlockSpec(memory_space=pl.ANY)],
        out_specs=vmem,
        compiler_params=pltpu.CompilerParams(vmem_limit_bytes=8 * MIB),
    )(t, mine, other_terms, denom, token)


def group(kind):
    groups = {}
    for p in range(16):
        for q in range(16):
            spot = dict(y=p // 4, h=p // 2 % 2, c=p % 2, x=q // 4, z=q % 4)
            key = tuple(spot[name] for name in "yhcxz" if name not in kind)
            groups.setdefault(key, []).append(p * 16 + q)
    return list(groups.values())


def exchange(value, kind):
    return lax.all_to_all(
        value, ("bulk", "occ"), 0, 0, axis_index_groups=group(kind), tiled=True
    )


def local(lambda_cd, integrals, other_terms, hole_energy, virtual_energy, pair_orbitals):
    core = lax.axis_index("bulk") % 2
    shift = bulk_shift
    own, other, g = pack(lambda_cd)
    z0 = shift("z0", own, dh=1)
    r0 = shift("r0", own, dy=-1)
    l0 = shift("l0", own, dy=1)
    sib = shift("sib", other, dc=1)
    g = stage(g, sib, cost=COSTS[0])
    l1 = shift("l1", after(sib, g), dy=1)
    r1 = shift("r1", after(sib, g), dy=-1)
    z1 = shift("z1", after(sib, g), dh=1)
    g = stage(g, r0, l0, cost=COSTS[2])
    f0 = shift("f0", after(r0, g), dy=-1)
    ints = jnp.transpose(after(integrals, g), (1, 0, 2))
    ints_other = lax.dynamic_slice_in_dim(ints, (1 - core) * C_HALF, C_HALF, axis=1)
    ints_sib = shift("ints", ints_other, dc=1).reshape(K_ALL, COLS)
    g = stage(g, r1, l1, cost=COSTS[3])
    f1 = shift("f1", after(l1, g), dy=1)
    g = stage(g, z0, cost=COSTS[4])
    zr0 = shift("zr0", after(z0, g), dy=-1)
    zl0 = shift("zl0", after(z0, g), dy=1)
    g = stage(g, z1, f0, f1, cost=COSTS[5])
    zr1 = shift("zr1", after(z1, g), dy=-1)
    zl1 = shift("zl1", after(z1, g), dy=1)
    g = stage(g, zr0, zl0, cost=COSTS[6])
    zf0 = shift("zf0", after(zl0, g), dy=1)
    ints = jnp.transpose(after(integrals, g), (1, 0, 2))
    ints_own = lax.dynamic_slice_in_dim(ints, core * C_HALF, C_HALF, axis=1)
    ints_own = ints_own.reshape(K_ALL, COLS)
    denom = denominators(
        after(hole_energy.reshape(1, -1), g), virtual_energy.reshape(1, -1), pair_orbitals.T
    )
    g = stage(g, zr1, ints_own, denom, cost=COSTS[7])
    zf1 = shift("zf1", after(zr1, g), dy=-1)

    near = {(0, 0, 0): own, (0, 0, 1): r0, (0, 0, 2): f0, (0, 0, 3): l0}
    near |= {(1, 0, 0): sib, (1, 0, 1): r1, (1, 0, 2): f1, (1, 0, 3): l1}
    far = {(0, 1, 0): z0, (0, 1, 1): zr0, (0, 1, 2): zf0, (0, 1, 3): zl0}
    far |= {(1, 1, 0): z1, (1, 1, 1): zr1, (1, 1, 2): zf1, (1, 1, 3): zl1}
    spots, mine, theirs = {}, [], []
    for k, pieces in enumerate((near, far)):
        for n, key in enumerate(pieces):
            spots[key] = (k, n * ROWS)
        pieces = jax.tree.leaves(list(pieces.values()))
        part = ladder(pieces, after(ints_sib, *mine, *theirs))
        theirs.append(shift("t%d" % k, part, dc=1))
        mine.append(ladder(pieces, after(ints_own, part)))
    by_x = combine(spots, mine, theirs)
    rows_x = jnp.sum(exchange(by_x, "x"), axis=0)
    by_z = jnp.broadcast_to(rows_x[None], (2,) + rows_x.shape).reshape(8, ROWS, COLS)
    by_z = exchange(by_z, "hz")
    direct, mixed = spread(by_z)
    swapped = exchange(mixed.reshape(8, 16, 128), "yc").reshape(128, 128)

    return final(swapped, direct, other_terms, denom, g)


def solution(mesh):
    placed = (
        P("bulk", "occ", None),
        P("occ", None, "bulk"),
        P("occ", "bulk"),
        P(),
        P(),
        P("occ", None),
    )
    return jax.shard_map(
        local, mesh=mesh, in_specs=placed, out_specs=P("occ", "bulk"), check_vma=False
    )
```

```python
import functools

import jax
import jax.numpy as jnp
from jax import lax
from jax.experimental import pallas as pl
from jax.experimental.pallas import tpu as pltpu
from jax.sharding import PartitionSpec as P

VW = 64
COLS = 256
ROWS = 32
HALF = 16
C_HALF = 8
D = 900
K_ALL = C_HALF * D
MIB = 1024 * 1024
COSTS = (10, 10, 10, 10, 10, 10, 10, 10)


def p_of(y, h, core):
    return ((y % 4) * 2 + h % 2) * 2 + core % 2


def here():
    p = lax.axis_index("bulk")
    return p // 4, (p // 2) % 2, p % 2


def bulk_shift(name, value, dy=0, dh=0, dc=0):
    pairs = []
    for y in range(4):
        for h in range(2):
            for core in range(2):
                pairs.append((p_of(y, h, core), p_of(y + dy, h + dh, core + dc)))
    with jax.named_scope(name):
        return lax.ppermute(value, "bulk", pairs)


def after(value, *others):
    return lax.optimization_barrier((value,) + others)[0]


def pack_kernel(lam_ref, own_ref, other_ref, token_ref):
    _, _, core = here()
    token_ref[...] = jnp.zeros_like(token_ref)
    n = ROWS * 16
    full = D // 128 * 128
    lam = jnp.transpose(lam_ref[...].astype(jnp.float32), (1, 0, 2))
    turned = jnp.concatenate([lam[C_HALF:], lam[:C_HALF]], axis=0)
    lam = jnp.where(core == 0, lam, turned).astype(jnp.bfloat16).reshape(n, D)
    main, rest = lam[:, :full], lam[:, full:]
    col = lax.broadcasted_iota(jnp.int32, (1, 1024), 1)
    row = lax.broadcasted_iota(jnp.int32, (1024, 1024), 0)
    weave = jnp.where(row == col % C_HALF * 128 + col // C_HALF, 1.0, 0.0)
    weave = weave.astype(jnp.bfloat16)
    tail = D - full
    source = lax.broadcasted_iota(jnp.int32, (tail, tail * C_HALF), 0)
    goal = lax.broadcasted_iota(jnp.int32, (tail, tail * C_HALF), 1)
    for k, out in enumerate((own_ref, other_ref)):
        first = k * 256
        blocks = [
            jnp.concatenate(
                [
                    main[first + i * ROWS : first + (i + 1) * ROWS, j * 128 : (j + 1) * 128]
                    for i in range(C_HALF)
                ],
                axis=1,
            )
            for j in range(full // 128)
        ]
        woven = jnp.dot(
            jnp.concatenate(blocks, axis=0), weave, preferred_element_type=jnp.float32
        ).astype(jnp.bfloat16)
        for j in range(full // 128):
            out[:, j * 1024 : (j + 1) * 1024] = woven[j * ROWS : (j + 1) * ROWS]
        total = jnp.zeros((ROWS, tail * C_HALF), jnp.float32)
        for i in range(C_HALF):
            put = jnp.where(goal == source * C_HALF + i, 1.0, 0.0).astype(jnp.bfloat16)
            total += jnp.dot(
                rest[first + i * ROWS : first + (i + 1) * ROWS],
                put,
                preferred_element_type=jnp.float32,
            )
        out[:, full * C_HALF :] = total.astype(jnp.bfloat16)


def pack(lam):
    piece = jax.ShapeDtypeStruct((ROWS, K_ALL), jnp.bfloat16)
    vmem = pl.BlockSpec(memory_space=pltpu.VMEM)
    return pl.pallas_call(
        pack_kernel,
        out_shape=[piece, piece, jax.ShapeDtypeStruct((8, 128), jnp.float32)],
        in_specs=[vmem],
        out_specs=[vmem] * 3,
        compiler_params=pltpu.CompilerParams(vmem_limit_bytes=24 * MIB),
        cost_estimate=pl.CostEstimate(
            flops=2 * 512 * 512 * 900, bytes_accessed=2 * MIB, transcendentals=0
        ),
    )(lam)


def stage_kernel(in_ref, out_ref):
    pass


def stage(token, *others, cost=10):
    place = pl.BlockSpec(memory_space=pl.ANY)
    return pl.pallas_call(
        stage_kernel,
        out_shape=jax.ShapeDtypeStruct((8, 128), jnp.float32),
        in_specs=[place],
        out_specs=place,
        input_output_aliases={0: 0},
        compiler_params=pltpu.CompilerParams(vmem_limit_bytes=MIB // 4),
        cost_estimate=pl.CostEstimate(
            flops=cost * 1_000_000_000, bytes_accessed=8192, transcendentals=0
        ),
    )(after(token, *others))


def ladder_kernel(*refs):
    pieces = refs[:-2]
    ints_ref, out_ref = refs[-2:]
    total = 0.0
    for start in range(0, K_ALL, 1024):
        part = slice(start, min(start + 1024, K_ALL))
        lam = jnp.concatenate([piece[:, part] for piece in pieces], axis=0)
        total += jnp.dot(lam, ints_ref[part, :], preferred_element_type=jnp.float32)
    out_ref[...] = total


def ladder(pieces, ints):
    m = sum(piece.shape[0] for piece in pieces)
    vmem = pl.BlockSpec(memory_space=pltpu.VMEM)
    return pl.pallas_call(
        ladder_kernel,
        out_shape=jax.ShapeDtypeStruct((m, COLS), jnp.float32),
        in_specs=[vmem] * (len(pieces) + 1),
        out_specs=vmem,
        compiler_params=pltpu.CompilerParams(vmem_limit_bytes=16 * MIB),
        cost_estimate=pl.CostEstimate(
            flops=2 * m * K_ALL * COLS,
            bytes_accessed=2 * K_ALL * (m + COLS),
            transcendentals=0,
        ),
    )(*pieces, ints)


def combine_kernel(spots, *refs):
    y, h, core = here()
    count = len(refs) // 2
    mine, theirs, out_ref = refs[:count], refs[count:-1], refs[-1]
    for (i, sh, sy), (k, row) in spots.items():
        other_k, other_row = spots[1 - i, sh, sy]
        zl = ((h + sh) % 2) * 2 + (core + i) % 2
        out_ref[(y + sy) % 4, zl] = (
            mine[k][row : row + ROWS, :] + theirs[other_k][other_row : other_row + ROWS, :]
        )


def combine(spots, mine, theirs):
    vmem = pl.BlockSpec(memory_space=pltpu.VMEM)
    return pl.pallas_call(
        functools.partial(combine_kernel, spots),
        out_shape=jax.ShapeDtypeStruct((4, 4, ROWS, COLS), jnp.float32),
        in_specs=[vmem] * (2 * len(mine)),
        out_specs=vmem,
        compiler_params=pltpu.CompilerParams(vmem_limit_bytes=8 * MIB),
    )(*mine, *theirs)


def spread_kernel(t_ref, here_ref, out_ref):
    _, h, _ = here()
    parts = []
    for dh in range(2):
        first = ((h + dh) % 2) * 4
        parts.append(t_ref[first] + t_ref[first + 1] + t_ref[first + 2] + t_ref[first + 3])
    here_ref[...] = parts[0]
    both = jnp.concatenate(parts, axis=0)
    none = jnp.zeros_like(both)
    row = lax.broadcasted_iota(jnp.int32, (64, COLS), 0)
    col = lax.broadcasted_iota(jnp.int32, (64, COLS), 1)
    target = ((row // 16) * 2 + h) * 2 + (row // 8) % 2
    total = jnp.zeros((64, 128), jnp.float32)
    for half in range(2):
        want = (half * 2 + (row // 4) % 2) * VW + target * 4 + row % 4
        total += lax.dot_general(
            jnp.where(col == want, 1.0, 0.0),
            jnp.concatenate([none, both] if half else [both, none], axis=0),
            (((1,), (1,)), ((), ())),
            precision=lax.Precision.HIGHEST,
            preferred_element_type=jnp.float32,
        )
    out_ref[...] = total


def spread(t):
    vmem = pl.BlockSpec(memory_space=pltpu.VMEM)
    return pl.pallas_call(
        spread_kernel,
        out_shape=[
            jax.ShapeDtypeStruct((ROWS, COLS), jnp.float32),
            jax.ShapeDtypeStruct((64, 128), jnp.float32),
        ],
        in_specs=[vmem],
        out_specs=[vmem] * 2,
        compiler_params=pltpu.CompilerParams(vmem_limit_bytes=8 * MIB),
    )(t)


def denom_kernel(hole_ref, virt_ref, pairs_ref, out_ref):
    y, h, core = here()
    exact = dict(precision=lax.Precision.HIGHEST, preferred_element_type=jnp.float32)
    row = lax.broadcasted_iota(jnp.int32, (VW, COLS), 0)
    col = lax.broadcasted_iota(jnp.int32, (VW, COLS), 1)
    own_a = ((y * 2 + h) * 2 + core) * 4 + col // VW
    pick_a = jnp.where(row == own_a, 1.0, 0.0)
    pick_b = jnp.where(row == col % VW, 1.0, 0.0)
    virtual = jnp.broadcast_to(virt_ref[...], (8, VW))
    virt_a = jnp.dot(virtual, pick_a, **exact)[:1]
    virt_b = jnp.dot(virtual, pick_b, **exact)[:1]
    count = hole_ref.shape[1]
    orbital = lax.broadcasted_iota(jnp.int32, (count, ROWS), 0)
    hole = jnp.broadcast_to(hole_ref[...], (8, count))
    diagonal = lax.broadcasted_iota(jnp.int32, (ROWS, ROWS), 0) == lax.broadcasted_iota(
        jnp.int32, (ROWS, ROWS), 1
    )
    holes = jnp.zeros((ROWS, 1), jnp.float32)
    for k in range(2):
        pick = jnp.where(orbital == pairs_ref[k : k + 1, :], 1.0, 0.0)
        energy = jnp.dot(hole, pick, **exact)[:1]
        holes += jnp.sum(jnp.where(diagonal, energy, 0.0), axis=1, keepdims=True)
    out_ref[...] = holes + virt_a + virt_b


def denominators(hole, virt, pairs):
    vmem = pl.BlockSpec(memory_space=pltpu.VMEM)
    return pl.pallas_call(
        denom_kernel,
        out_shape=jax.ShapeDtypeStruct((ROWS, COLS), jnp.float32),
        in_specs=[vmem] * 3,
        out_specs=vmem,
        compiler_params=pltpu.CompilerParams(vmem_limit_bytes=8 * MIB),
    )(hole, virt, pairs)


def final_kernel(t_ref, mine_ref, other_ref, denom_ref, token_ref, out_ref):
    _, h, _ = here()
    exact = dict(precision=lax.Precision.HIGHEST, preferred_element_type=jnp.float32)
    row = lax.broadcasted_iota(jnp.int32, (64, COLS), 0)
    col = lax.broadcasted_iota(jnp.int32, (64, COLS), 1)
    swapped = jnp.zeros((ROWS, COLS), jnp.float32)
    t = t_ref[...].T
    for half in range(2):
        for dh in range(2):
            source = ((row // 16) * 2 + (h + dh) % 2) * 2 + (row // 8) % 2
            goal = (row % 4) * VW + source * 4 + half * 2 + (row // 4) % 2
            put = jnp.where(col == goal, 1.0, 0.0)
            first = (half * 2 + dh) * ROWS
            swapped += jnp.dot(t[first : first + ROWS], put, **exact)
    antisym = mine_ref[...] - swapped
    out_ref[...] = -(other_ref[...].astype(jnp.float32) + 0.5 * antisym) / denom_ref[...]


def final(t, mine, other_terms, denom, token):
    vmem = pl.BlockSpec(memory_space=pltpu.VMEM)
    return pl.pallas_call(
        final_kernel,
        out_shape=jax.ShapeDtypeStruct((ROWS, COLS), jnp.float32),
        in_specs=[vmem] * 4 + [pl.BlockSpec(memory_space=pl.ANY)],
        out_specs=vmem,
        compiler_params=pltpu.CompilerParams(vmem_limit_bytes=8 * MIB),
    )(t, mine, other_terms, denom, token)


def group(kind):
    groups = {}
    for p in range(16):
        for q in range(16):
            spot = dict(y=p // 4, h=p // 2 % 2, c=p % 2, x=q // 4, z=q % 4)
            key = tuple(spot[name] for name in "yhcxz" if name not in kind)
            groups.setdefault(key, []).append(p * 16 + q)
    return list(groups.values())


def exchange(value, kind):
    return lax.all_to_all(
        value, ("bulk", "occ"), 0, 0, axis_index_groups=group(kind), tiled=True
    )


def local(lambda_cd, integrals, other_terms, hole_energy, virtual_energy, pair_orbitals):
    core = lax.axis_index("bulk") % 2
    shift = bulk_shift
    own, other, g = pack(lambda_cd)
    z0 = shift("z0", own, dh=1)
    r0 = shift("r0", own, dy=-1)
    l0 = shift("l0", own, dy=1)
    sib = shift("sib", other, dc=1)
    g = stage(g, sib, cost=COSTS[0])
    l1 = shift("l1", after(sib, g), dy=1)
    r1 = shift("r1", after(sib, g), dy=-1)
    z1 = shift("z1", after(sib, g), dh=1)
    g = stage(g, r0, l0, cost=COSTS[2])
    f0 = shift("f0", after(r0, g), dy=-1)
    ints = jnp.transpose(after(integrals, g), (1, 0, 2))
    ints_other = lax.dynamic_slice_in_dim(ints, (1 - core) * C_HALF, C_HALF, axis=1)
    ints_sib = shift("ints", ints_other, dc=1).reshape(K_ALL, COLS)
    g = stage(g, r1, l1, cost=COSTS[3])
    f1 = shift("f1", after(l1, g), dy=1)
    g = stage(g, z0, f0, cost=COSTS[4])
    zr0 = shift("zr0", after(z0, g), dy=-1)
    zl0 = shift("zl0", after(z0, g), dy=1)
    g = stage(g, z1, f1, cost=COSTS[5])
    zr1 = shift("zr1", after(z1, g), dy=-1)
    zl1 = shift("zl1", after(z1, g), dy=1)
    g = stage(g, zr0, zl0, cost=COSTS[6])
    zf0 = shift("zf0", after(zl0, g), dy=1)
    ints = jnp.transpose(after(integrals, g), (1, 0, 2))
    ints_own = lax.dynamic_slice_in_dim(ints, core * C_HALF, C_HALF, axis=1)
    ints_own = ints_own.reshape(K_ALL, COLS)
    denom = denominators(
        after(hole_energy.reshape(1, -1), g), virtual_energy.reshape(1, -1), pair_orbitals.T
    )
    g = stage(g, zr1, ints_own, denom, cost=COSTS[7])
    zf1 = shift("zf1", after(zr1, g), dy=-1)

    near = {(0, 0, 0): own, (0, 0, 1): r0, (0, 0, 2): f0, (0, 0, 3): l0}
    near |= {(1, 0, 0): sib, (1, 0, 1): r1, (1, 0, 2): f1, (1, 0, 3): l1}
    far = {(0, 1, 0): z0, (0, 1, 1): zr0, (0, 1, 2): zf0, (0, 1, 3): zl0}
    far |= {(1, 1, 0): z1, (1, 1, 1): zr1, (1, 1, 2): zf1, (1, 1, 3): zl1}
    spots, mine, theirs = {}, [], []
    for k, pieces in enumerate((near, far)):
        for n, key in enumerate(pieces):
            spots[key] = (k, n * ROWS)
        pieces = jax.tree.leaves(list(pieces.values()))
        part = ladder(pieces, after(ints_sib, *mine, *theirs))
        theirs.append(shift("t%d" % k, part, dc=1))
        mine.append(ladder(pieces, after(ints_own, part)))
    by_x = combine(spots, mine, theirs)
    rows_x = jnp.sum(exchange(by_x, "x"), axis=0)
    by_z = jnp.broadcast_to(rows_x[None], (2,) + rows_x.shape).reshape(8, ROWS, COLS)
    by_z = exchange(by_z, "hz")
    direct, mixed = spread(by_z)
    swapped = exchange(mixed.reshape(8, 8, 128), "yc").reshape(64, 128)

    return final(swapped, direct, other_terms, denom, g)


def solution(mesh):
    placed = (
        P("bulk", "occ", None),
        P("occ", None, "bulk"),
        P("occ", "bulk"),
        P(),
        P(),
        P("occ", None),
    )
    return jax.shard_map(
        local, mesh=mesh, in_specs=placed, out_specs=P("occ", "bulk"), check_vma=False
    )
```
